128 devices in a mesh: dp: 8 (over y_lo, x), ctx: 16 (over z, y_hi, core).
Axes of the slice: x: 4, y: 4 (y_hi: 2, y_lo: 2; y = y_hi * 2 + y_lo), z: 4, core: 2. Of those that a mesh axis runs over, the one named last changes fastest.
Arguments:
- query_one: bfloat16 [16384, 4096], P(('dp', 'ctx')), parts along dimension 0, may hold values from -64 to 64
- query_two: bfloat16 [16384, 4096], P(('dp', 'ctx')), parts along dimension 0, may hold values from -64 to 64
- shared_keys: bfloat16 [16384, 512], P(('dp', 'ctx')), parts along dimension 0, may hold values from -8 to 8
- common_values: bfloat16 [16384, 512], P(('dp', 'ctx')), parts along dimension 0, may hold values from -6 to 6
- cotangent_one: bfloat16 [16384, 4096], P(('dp', 'ctx')), parts along dimension 0, may hold values from -96 to 96
- cotangent_two: bfloat16 [16384, 4096], P(('dp', 'ctx')), parts along dimension 0, may hold values from -96 to 96
- span_order: int32 [256], P('dp'), parts along dimension 0, may hold values from 0 to 31, each once
- lengths: int32 [64], P('dp'), parts along dimension 0, may hold values from 1 to 1024, 2048 in all
Outputs:
- query_grad_one: bfloat16 [16384, 4096], P(('dp', 'ctx')), parts along dimension 0
- query_grad_two: bfloat16 [16384, 4096], P(('dp', 'ctx')), parts along dimension 0
- key_grad: bfloat16 [16384, 512], P(('dp', 'ctx')), parts along dimension 0
- value_grad: bfloat16 [16384, 512], P(('dp', 'ctx')), parts along dimension 0
The draws below stay inside these ranges and needn't reach their ends.
There are 8 independent parts, one for each index of `dp`. The reference program is written for one: setup_inputs(seed, part) draws one part's arguments, and reference() takes and returns one part's arrays. A program takes and returns all parts, laid end to end along the dimension named above; each array names one. Nothing has to cross between parts.
Inputs may be any that keep to these rules, and one draw needn't show every extreme that they name: `span_order`: a permutation. `lengths`: they sum to 2048; the largest is exactly 1024.
All inputs are finite; a program needn't handle non-finite values.
Results may differ from the reference program's by a relative error of at most 0.0075.
Values may be sent and summed in bfloat16 or wider, within the bound.
No kernel may reach another device: no remote copies, remote signals or barrier semaphores. Data moves between devices by JAX's collectives and lax.ppermute only.
A program may use at most 320 MiB of HBM per device.

```python
import math
import jax
import jax.numpy as jnp
import numpy as np
from jax import lax

HEAD_SIZE = 128
KEY_VALUE_HEADS = 4
QUERY_PER_KEY = 8
NDOC = 8
QUERY_HEADS = 32
HALF = 64
SEQUENCE_TOKENS = 2048
MOST = 1024
N_CTX = 16


def key_base(key):
    unscaled_input = jax.random.normal(key, (SEQUENCE_TOKENS, KEY_VALUE_HEADS * HEAD_SIZE), jnp.float32)
    rows = jnp.arange(SEQUENCE_TOKENS)
    paired = (rows % 8 == 0)[:, None]
    mixed = jnp.where(paired, unscaled_input, unscaled_input)
    return jnp.clip(mixed, -8.0, 8.0)


def query_draw(key, salt, strong):
    key = jax.random.fold_in(key, salt)
    drawn = jax.random.normal(key, (SEQUENCE_TOKENS, QUERY_HEADS * HEAD_SIZE), jnp.float32)
    rows = jnp.arange(SEQUENCE_TOKENS)
    chosen = (rows % 8 == 1)[:, None].astype(jnp.float32) * strong
    return drawn * (1.0 - chosen)


def draw_shared_keys(key, part):
    return key_base(key).astype(jnp.bfloat16)


def draw_query_one(key, part):
    strong = 0.0
    return query_draw(key, 11, strong).astype(jnp.bfloat16)


def draw_query_two(key, part):
    strong = 0.0
    return query_draw(key, 23, strong).astype(jnp.bfloat16)


def shard_levels(stream_key, dims, shards, low, top_value):
    level, own = 1.0, jax.random.fold_in(stream_key, 6)
    for position, blocks in shards:
        heights = jnp.exp(jax.random.uniform(jax.random.fold_in(own, position), (blocks,), jnp.float32, low / len(shards), top_value / len(shards)))
        level = level * jnp.repeat(heights, dims[position] // blocks).reshape([-1 if axis == position else 1 for axis in range(len(dims))])
    return level


def profile(count, total, limit, slope):
    portions = [(1 << 20) // math.isqrt(grade ** slope) + 1 for grade in range(2, count + 1)]
    surplus, given = total - limit - (count - 1), [1] * (count - 1)
    while surplus > 0:
        candidates = [i for i in range(count - 1) if given[i] < limit]
        whole, left = sum([portions[i] for i in candidates]), surplus
        for i in candidates:
            extra = min(limit - given[i], max(1, left * portions[i] // whole), surplus)
            given[i] = given[i] + extra
            surplus = surplus - extra
    return np.array([limit] + given)


def uneven_parts(stream_key, count, total, bound, slope):
    if count == 2:
        one = jax.random.randint(stream_key, (), max(1, total - bound), min(bound, total - 1) + 1)
        return jnp.stack([one, total - one])
    sizes = jnp.asarray(profile(count, total, bound, slope), jnp.int32)
    twos = (count - 1) // 2
    giver, sink = sizes[1:1 + 2 * twos:2], sizes[2:2 + 2 * twos:2]
    slack = jnp.minimum(giver - 1, bound - sink)
    shifted = jax.random.randint(jax.random.fold_in(stream_key, 1), (twos,), 0, 1 << 20) % (slack + 1)
    sizes = sizes.at[1:1 + 2 * twos:2].set(giver - shifted).at[2:2 + 2 * twos:2].set(sink + shifted)
    return sizes[jax.random.permutation(jax.random.fold_in(stream_key, 2), count)]


def scatter_about(rng, dims, deviation, limit, pieces=(), kind=jnp.bfloat16):
    drawn = deviation * jax.random.normal(rng, dims, jnp.float32)
    if pieces:
        drawn = drawn * shard_levels(rng, dims, pieces, -0.22, 0.18)
    return jnp.clip(drawn, -limit, limit).astype(kind)


def setup_inputs(seed: int = 0, part: int = 0) -> dict:
    seeds = jax.random.split(jax.random.key(seed), 9)
    part_keys = jax.random.split(jax.random.fold_in(seeds[8], part), 9)
    query_one = draw_query_one(jax.random.fold_in(jax.random.fold_in(seeds[8], part), 71), part)
    query_two = draw_query_two(jax.random.fold_in(jax.random.fold_in(seeds[8], part), 71), part)
    shared_keys = draw_shared_keys(jax.random.fold_in(jax.random.fold_in(seeds[8], part), 71), part)
    common_values = scatter_about(part_keys[3], (SEQUENCE_TOKENS, KEY_VALUE_HEADS * HEAD_SIZE), 1.0, 6.0, ((0, 16),))
    cotangent_one = scatter_about(part_keys[4], (SEQUENCE_TOKENS, QUERY_HEADS * HEAD_SIZE), 16.0, 96.0, ((0, 16),))
    cotangent_two = scatter_about(part_keys[5], (SEQUENCE_TOKENS, QUERY_HEADS * HEAD_SIZE), 16.0, 96.0, ((0, 16),))
    span_order = jax.random.permutation(part_keys[6], 2 * N_CTX).astype(jnp.int32)
    lengths = uneven_parts(part_keys[7], NDOC, SEQUENCE_TOKENS, MOST, 2).astype(jnp.int32)
    return {"query_one": query_one, "query_two": query_two, "shared_keys": shared_keys, "common_values": common_values, "cotangent_one": cotangent_one, "cotangent_two": cotangent_two, "span_order": span_order, "lengths": lengths}


def token_positions(span_order):
    rows = jnp.arange(SEQUENCE_TOKENS, dtype=jnp.int32)
    return (span_order[rows // HALF] * HALF + rows % HALF).astype(jnp.int32)


def documents_of(positions, lengths):
    ends = jnp.cumsum(lengths).astype(jnp.int32)
    return jnp.sum((positions[:, None] >= ends[None, :]).astype(jnp.int32), axis=1)


def layer_grads(queries, key_rows, values, cotangent, visible):
    scale = HEAD_SIZE ** -0.5
    query_parts, key_parts, value_parts = [], [], []
    for group_width in range(KEY_VALUE_HEADS):
        query_block = queries[:, group_width * QUERY_PER_KEY * HEAD_SIZE:(group_width + 1) * QUERY_PER_KEY * HEAD_SIZE].reshape(SEQUENCE_TOKENS, QUERY_PER_KEY, HEAD_SIZE).astype(jnp.float32)
        cot_block = cotangent[:, group_width * QUERY_PER_KEY * HEAD_SIZE:(group_width + 1) * QUERY_PER_KEY * HEAD_SIZE].reshape(SEQUENCE_TOKENS, QUERY_PER_KEY, HEAD_SIZE).astype(jnp.float32)
        key_block = key_rows[:, group_width * HEAD_SIZE:(group_width + 1) * HEAD_SIZE].astype(jnp.float32)
        value_block = values[:, group_width * HEAD_SIZE:(group_width + 1) * HEAD_SIZE].astype(jnp.float32)
        scores = jnp.einsum("thd,kd->htk", query_block, key_block) * scale
        scores = jnp.where(visible[None], scores, -1e30)
        peak = jnp.max(scores, axis=-1, keepdims=True)
        expo = jnp.exp(scores - peak)
        probs = expo / jnp.sum(expo, axis=-1, keepdims=True)
        probs_low = lax.optimization_barrier(probs.astype(jnp.bfloat16)).astype(jnp.float32)
        dprobs = jnp.einsum("thd,kd->htk", cot_block, value_block)
        dsum = jnp.sum(probs * dprobs, axis=-1, keepdims=True)
        dscores = probs * (dprobs - dsum)
        dscores_low = lax.optimization_barrier((dscores * scale).astype(jnp.bfloat16)).astype(jnp.float32)
        query_parts.append(jnp.einsum("htk,kd->thd", dscores_low, key_block).reshape(SEQUENCE_TOKENS, QUERY_PER_KEY * HEAD_SIZE))
        key_parts.append(jnp.einsum("htk,thd->kd", dscores_low, query_block))
        value_parts.append(jnp.einsum("htk,thd->kd", probs_low, cot_block))
    return (jnp.concatenate(query_parts, axis=1), jnp.concatenate(key_parts, axis=1), jnp.concatenate(value_parts, axis=1))


def reference(query_one, query_two, shared_keys, common_values, cotangent_one, cotangent_two, span_order, lengths):
    positions = token_positions(span_order)
    documents = documents_of(positions, lengths)
    visible = (positions[None, :] <= positions[:, None]) & (documents[None, :] == documents[:, None])
    grad_q1, grad_k1, grad_v1 = layer_grads(query_one, shared_keys, common_values, cotangent_one, visible)
    grad_q2, grad_k2, grad_v2 = layer_grads(query_two, shared_keys, common_values, cotangent_two, visible)
    return (grad_q1.astype(jnp.bfloat16), grad_q2.astype(jnp.bfloat16), (grad_k1 + grad_k2).astype(jnp.bfloat16), (grad_v1 + grad_v2).astype(jnp.bfloat16))
```

```python
import math

import jax
import jax.numpy as jnp
from jax import lax
from jax.experimental import pallas as pl
from jax.experimental.pallas import tpu as pltpu
from jax.sharding import PartitionSpec as P

HEAD = 128
KEY_VALUE_HEADS = 4
QUERY_PER_KEY = 8
HALF = 64
MOST = 1024
NEG = -1e30
SCALE = HEAD**-0.5
LOG2E = math.log2(math.e)
Z, Y = 4, 2
CHIPS = Z * Y
TOKENS = 2048
BLOCKS = TOKENS // HALF
HEADS_HERE = KEY_VALUE_HEADS // 2
WIDTH = QUERY_PER_KEY * HEAD
ROWS = 2 * QUERY_PER_KEY * HALF
TILE = 256
PAD = TILE
STEPS = -(-(MOST + HALF) // TILE)
LANES = 512
CHUNKS = ROWS // LANES
OFFSETS = ((0, 0), (0, 1), (-1, 0), (-1, 1), (1, 0), (1, 1), (-2, 0), (2, 1))


def device_of(z, y, core):
    return ((z % Z) * Y + y % Y) * 2 + core


def moves(dz, dy, dcore):
    return [
        (device_of(z, y, c), device_of(z + dz, y + dy, (c + dcore) % 2))
        for z in range(Z)
        for y in range(Y)
        for c in range(2)
    ]


def send(x, dz, dy, dcore=0):
    return lax.ppermute(x, "ctx", moves(dz, dy, dcore))


def block_grads(position, lens, qs, gs, dqs, ks, vs, dk, dv, es, dps, ms, dqt, qst, gst, bias):
    token = lax.broadcasted_iota(jnp.int32, (1, 128), 1) % HALF
    where = position * HALF + token
    starts = jnp.zeros((1, 128), jnp.int32)
    low = jnp.int32(0)
    end = jnp.int32(0)
    for k in range(lens.shape[0]):
        end = end + lens[k]
        starts = jnp.where(where >= end, end, starts)
        low = jnp.where(position * HALF >= end, end, low)
    stop = (position + 1) * HALF
    steps = (stop - low + TILE - 1) // TILE
    for layer in range(2):
        for h in range(QUERY_PER_KEY):
            r = (layer * QUERY_PER_KEY + h) * HALF
            qst[r : r + HALF, :] = qs[layer][:, h * HEAD : (h + 1) * HEAD]
            gst[r : r + HALF, :] = gs[layer][:, h * HEAD : (h + 1) * HEAD]
    by_head = (((1,), (1,)), ((), ()))

    def scores(t, carry):
        base = stop - (t + 1) * TILE
        row = pl.multiple_of(base + PAD, HALF)
        at = pl.multiple_of(t * TILE, TILE)
        kt = ks[pl.ds(row, TILE), :]
        vt = vs[pl.ds(row, TILE), :]
        key = base + lax.broadcasted_iota(jnp.int32, (TILE, 128), 0)
        bias[...] = jnp.where((key <= where) & (key >= starts), 0.0, NEG)
        out = []
        for c in range(CHUNKS):
            top, total, mean = carry[c]
            sl = slice(c * LANES, (c + 1) * LANES)
            s = lax.dot_general(kt, qst[sl, :], by_head, preferred_element_type=jnp.float32)
            dp = lax.dot_general(vt, gst[sl, :], by_head, preferred_element_type=jnp.float32)
            s = s * (SCALE * LOG2E) + jnp.concatenate([bias[...]] * (LANES // 128), axis=1)
            now = jnp.maximum(top, jnp.max(s, axis=0, keepdims=True))
            e = jnp.exp2(s - now)
            shrink = jnp.exp2(top - now)
            total = total * shrink + jnp.sum(e, axis=0, keepdims=True)
            mean = mean * shrink + jnp.sum(e * dp, axis=0, keepdims=True)
            es[pl.ds(at, TILE), sl] = e
            dps[pl.ds(at, TILE), sl] = dp
            ms[t, :, sl] = jnp.broadcast_to(now, (8, LANES))
            out.append((now, total, mean))
        return tuple(out)

    zero = jnp.zeros((1, LANES), jnp.float32)
    found = lax.fori_loop(0, steps, scores, tuple((zero + NEG, zero, zero) for _ in range(CHUNKS)))
    inverse = [1.0 / f[1] for f in found]
    dsum = [f[2] * i for f, i in zip(found, inverse)]
    dqt[...] = jnp.zeros_like(dqt)

    def grads(t, _):
        row = pl.multiple_of(stop - (t + 1) * TILE + PAD, HALF)
        at = pl.multiple_of(t * TILE, TILE)
        kt = ks[pl.ds(row, TILE), :]
        dvt = dv[pl.ds(row, TILE), :]
        dkt = dk[pl.ds(row, TILE), :]
        for c in range(CHUNKS):
            sl = slice(c * LANES, (c + 1) * LANES)
            p = es[pl.ds(at, TILE), sl] * (jnp.exp2(ms[t, 0:1, sl] - found[c][0]) * inverse[c])
            ds = (p * (dps[pl.ds(at, TILE), sl] - dsum[c]) * SCALE).astype(jnp.bfloat16)
            dvt = dvt + jnp.dot(p.astype(jnp.bfloat16), gst[sl, :], preferred_element_type=jnp.float32)
            dkt = dkt + jnp.dot(ds, qst[sl, :], preferred_element_type=jnp.float32)
            dqt[:, sl] += lax.dot_general(kt, ds, (((0,), (0,)), ((), ())), preferred_element_type=jnp.float32)
        dv[pl.ds(row, TILE), :] = dvt
        dk[pl.ds(row, TILE), :] = dkt
        return 0

    lax.fori_loop(0, steps, grads, 0)
    for layer in range(2):
        for h in range(0, QUERY_PER_KEY, 2):
            r = (layer * QUERY_PER_KEY + h) * HALF
            x = dqt[:, r : r + 128].astype(jnp.bfloat16).T
            dqs[layer][:, h * HEAD : (h + 1) * HEAD] = x[:HALF]
            dqs[layer][:, (h + 1) * HEAD : (h + 2) * HEAD] = x[HALF:]


def kernel(core, table, lens, *refs):
    own, other, pieces, outs, total, scratch = refs[:4], refs[4:8], refs[8:16], refs[16:20], refs[20], refs[21:]
    ks, vs, dk, dv = scratch[:4]
    step = pl.program_id(0)

    @pl.when(step == 0)
    def _():
        ks[:PAD, :] = jnp.zeros((PAD, HEAD), jnp.bfloat16)
        vs[:PAD, :] = jnp.zeros((PAD, HEAD), jnp.bfloat16)
        dk[...] = jnp.zeros_like(dk)
        dv[...] = jnp.zeros_like(dv)
        for i in range(BLOCKS):
            p = pl.multiple_of(table[i] * HALF + PAD, HALF)
            x = pieces[i // 4][(i % 4) * HALF : (i % 4 + 1) * HALF, :]
            ks[pl.ds(p, HALF), :] = x[:, :HEAD]
            vs[pl.ds(p, HALF), :] = x[:, HEAD:]

    block_grads(table[step], lens, own[:2], own[2:], outs[:2], *scratch)
    block_grads(table[step + 2], lens, other[:2], other[2:], outs[2:], *scratch)

    @pl.when(step == 1)
    def _():
        for i in range(BLOCKS):
            p = pl.multiple_of(table[i] * HALF + PAD, HALF)
            rows = slice((i % 4) * HALF, (i % 4 + 1) * HALF)
            total[i // 4, rows, :HEAD] = dk[pl.ds(p, HALF), :].astype(jnp.bfloat16)
            total[i // 4, rows, HEAD:] = dv[pl.ds(p, HALF), :].astype(jnp.bfloat16)


def head_grads(g, core, table, lens, own, other, pieces):
    return pl.pallas_call(
        kernel,
        grid_spec=pltpu.PrefetchScalarGridSpec(
            num_scalar_prefetch=3,
            grid=(2,),
            in_specs=[pl.BlockSpec((HALF, WIDTH), lambda s, core, *_: (s, core[0] * HEADS_HERE + g))] * 4
            + [pl.BlockSpec((HALF, WIDTH), lambda s, *_: (s, g))] * 4
            + [pl.BlockSpec((4 * HALF, 2 * HEAD), lambda s, *_: (0, 0))] * CHIPS,
            out_specs=[pl.BlockSpec((HALF, WIDTH), lambda s, *_: (s, 0))] * 4
            + [pl.BlockSpec((CHIPS, 4 * HALF, 2 * HEAD), lambda s, *_: (0, 0, 0))],
            scratch_shapes=[
                pltpu.VMEM((TOKENS + PAD, HEAD), jnp.bfloat16),
                pltpu.VMEM((TOKENS + PAD, HEAD), jnp.bfloat16),
                pltpu.VMEM((TOKENS + PAD, HEAD), jnp.float32),
                pltpu.VMEM((TOKENS + PAD, HEAD), jnp.float32),
                pltpu.VMEM((STEPS * TILE, ROWS), jnp.float32),
                pltpu.VMEM((STEPS * TILE, ROWS), jnp.float32),
                pltpu.VMEM((STEPS, 8, ROWS), jnp.float32),
                pltpu.VMEM((HEAD, ROWS), jnp.float32),
                pltpu.VMEM((ROWS, HEAD), jnp.bfloat16),
                pltpu.VMEM((ROWS, HEAD), jnp.bfloat16),
                pltpu.VMEM((TILE, 128), jnp.float32),
            ],
        ),
        out_shape=[jax.ShapeDtypeStruct((2 * HALF, WIDTH), jnp.bfloat16)] * 4
        + [jax.ShapeDtypeStruct((CHIPS, 4 * HALF, 2 * HEAD), jnp.bfloat16)],
        compiler_params=pltpu.CompilerParams(
            dimension_semantics=("arbitrary",), vmem_limit_bytes=36 * 2**20
        ),
        cost_estimate=pl.CostEstimate(flops=12 * 10**9, bytes_accessed=6 * 2**20, transcendentals=2 * 10**6),
        name="block_grads",
    )(core, table, lens, *own, *other, *pieces)


def gather(x):
    y = send(x, 0, 1)
    rx, lx = send(x, 1, 0), send(x, -1, 0)
    rxx = send(rx, 1, 0)
    ry, ly = send(y, 1, 0), send(y, -1, 0)
    lyy = send(ly, -1, 0)
    return x, y, rx, ry, lx, ly, rxx, lyy


def add(*xs):
    total = xs[0].astype(jnp.float32)
    for x in xs[1:]:
        total = total + x.astype(jnp.float32)
    return total


def scatter(w):
    low = lambda x: x.astype(jnp.bfloat16)
    a = send(w[6], -1, 0)
    b = send(w[7], 1, 0)
    d = send(w[4], 1, 0)
    e = send(w[3], -1, 0)
    f = send(low(add(w[2], a)), -1, 0)
    h = send(low(add(w[5], b)), 1, 0)
    i = send(low(add(w[1], e, h)), 0, 1)
    return add(w[0], d, f, i)


def local(query_one, query_two, keys, values, cotangent_one, cotangent_two, span_order, lengths):
    device = lax.axis_index("ctx")
    core = device % 2
    z, y = device // 2 // Y, device // 2 % Y
    half = HEADS_HERE * HEAD

    def mine(x, who, width):
        return lax.dynamic_slice(x, (0, who * width), (x.shape[0], width))

    def pairs(who):
        k, v = mine(keys, who, half), mine(values, who, half)
        return jnp.concatenate(
            [p[:, g * HEAD : (g + 1) * HEAD] for g in range(HEADS_HERE) for p in (k, v)], axis=1
        )

    here, there = pairs(core), send(pairs(1 - core), 0, 0, 1)
    xs = [
        jnp.concatenate([p[:, g * 2 * HEAD : (g + 1) * 2 * HEAD] for p in (here, there)], axis=0)
        for g in range(HEADS_HERE)
    ]
    slots = []
    for dz, dy in OFFSETS:
        chip = (z + dz + Z) % Z * Y + (y + dy) % Y
        slots += [4 * chip + 2 * core, 4 * chip + 2 * core + 1]
        slots += [4 * chip + 2 * (1 - core), 4 * chip + 2 * (1 - core) + 1]
    table = jnp.take(span_order, jnp.stack(slots))
    core_of = jnp.reshape(core, (1,))
    own = (query_one, query_two, cotangent_one, cotangent_two)
    other = [send(mine(x, 1 - core, HEADS_HERE * WIDTH), 0, 0, 1) for x in own]
    kept, got, sums = [[], []], [[], []], []
    for g in range(HEADS_HERE):
        pieces = gather(xs[g])
        *dqs, total = head_grads(g, core_of, table, lengths, own, other, pieces)
        for layer in range(2):
            kept[layer].append(dqs[layer])
            got[layer].append(send(dqs[2 + layer], 0, 0, 1))
        sums.append(scatter(total).astype(jnp.bfloat16))
    sums = jnp.stack(sums, axis=1)
    rows = 2 * HALF
    kv_kept, kv_got = sums[:rows], send(sums[rows:], 0, 0, 1)

    def whole(a, b):
        return jnp.where(core == 0, jnp.concatenate(a + b, axis=1), jnp.concatenate(b + a, axis=1))

    def heads(x, k):
        return [x[:, g, k * HEAD : (k + 1) * HEAD] for g in range(HEADS_HERE)]

    return (
        whole(kept[0], got[0]),
        whole(kept[1], got[1]),
        whole(heads(kv_kept, 0), heads(kv_got, 0)),
        whole(heads(kv_kept, 1), heads(kv_got, 1)),
    )


def solution(mesh):
    rows = P(("dp", "ctx"), None)
    return jax.shard_map(
        local,
        mesh=mesh,
        in_specs=(rows,) * 6 + (P("dp"), P("dp")),
        out_specs=(rows,) * 4,
        check_vma=False,
    )
```

```python
import math

import jax
import jax.numpy as jnp
from jax import lax
from jax.experimental import pallas as pl
from jax.experimental.pallas import tpu as pltpu
from jax.sharding import PartitionSpec as P

HEAD = 128
KEY_VALUE_HEADS = 4
QUERY_PER_KEY = 8
HALF = 64
MOST = 1024
NEG = -1e30
SCALE = HEAD**-0.5
LOG2E = math.log2(math.e)
Z, Y = 4, 2
CHIPS = Z * Y
TOKENS = 2048
BLOCKS = TOKENS // HALF
SHARE = KEY_VALUE_HEADS // 2
HEADS = 1
PART = HEADS * HEAD
WIDTH = QUERY_PER_KEY * HEAD
ROWS = 2 * QUERY_PER_KEY * HALF
TILE = 512
TAILS = (128, 256, 384)
PAD = TILE
KEYS = (MOST + HALF + TAILS[0]) // TAILS[0] * TAILS[0]
LANES = 512
CHUNKS = [(g, c) for g in range(HEADS) for c in range(ROWS // LANES)]


def device_of(z, y, core):
    return ((z % Z) * Y + y % Y) * 2 + core


def swap(x):
    return lax.ppermute(x, "ctx", [(d, d ^ 1) for d in range(CHIPS * 2)])


def exchange(x):
    groups = [[device_of(z, y, c) for z in range(Z) for y in range(Y)] for c in range(2)]
    return lax.all_to_all(x, "ctx", 0, 0, axis_index_groups=groups, tiled=True)


def block_grads(position, lens, qs, gs, dqs, ks, vs, dk, dv, es, dps, ms, dqt, qst, gst, bias):
    token = lax.broadcasted_iota(jnp.int32, (1, 128), 1) % HALF
    where = position * HALF + token
    starts = jnp.zeros((1, 128), jnp.int32)
    low = jnp.int32(0)
    end = jnp.int32(0)
    for k in range(lens.shape[0]):
        end = end + lens[k]
        starts = jnp.where(where >= end, end, starts)
        low = jnp.where(position * HALF >= end, end, low)
    stop = (position + 1) * HALF
    count = stop - low
    steps = (count + TILE - TAILS[-1] - 1) // TILE
    rest = count - steps * TILE
    short = [(low < rest) & (rest <= size) for low, size in zip((0, *TAILS), TAILS)]
    for g in range(HEADS):
        for layer in range(2):
            for h in range(QUERY_PER_KEY):
                r = (layer * QUERY_PER_KEY + h) * HALF
                col = (g * QUERY_PER_KEY + h) * HEAD
                qst[g, r : r + HALF, :] = qs[layer][:, col : col + HEAD]
                gst[g, r : r + HALF, :] = gs[layer][:, col : col + HEAD]
    by_head = (((1,), (1,)), ((), ()))

    def scores(t, at, size, carry):
        base = stop - at - size
        row = pl.multiple_of(base + PAD, HALF)
        key = base + lax.broadcasted_iota(jnp.int32, (size, 128), 0)
        bias[:size, :] = jnp.where((key <= where) & (key >= starts), 0.0, NEG)
        out = []
        for i, (g, c) in enumerate(CHUNKS):
            top, total, mean = carry[i]
            sl = slice(c * LANES, (c + 1) * LANES)
            to = slice(i * LANES, (i + 1) * LANES)
            kt = ks[g, pl.ds(row, size), :]
            vt = vs[g, pl.ds(row, size), :]
            s = lax.dot_general(kt, qst[g, sl, :], by_head, preferred_element_type=jnp.float32)
            dp = lax.dot_general(vt, gst[g, sl, :], by_head, preferred_element_type=jnp.float32)
            s = s * (SCALE * LOG2E) + jnp.concatenate([bias[:size, :]] * (LANES // 128), axis=1)
            now = jnp.maximum(top, jnp.max(s, axis=0, keepdims=True))
            e = jnp.exp2(s - now)
            shrink = jnp.exp2(top - now)
            total = total * shrink + jnp.sum(e, axis=0, keepdims=True)
            mean = mean * shrink + jnp.sum(e * dp, axis=0, keepdims=True)
            es[pl.ds(at, size), to] = e
            dps[pl.ds(at, size), to] = dp
            ms[t, :, to] = jnp.broadcast_to(now, (8, LANES))
            out.append((now, total, mean))
        return tuple(out)

    zero = jnp.zeros((1, LANES), jnp.float32)
    found = tuple((zero + NEG, zero, zero) for _ in CHUNKS)
    at_rest = pl.multiple_of(steps * TILE, TILE)
    found = lax.fori_loop(0, steps, lambda t, f: scores(t, pl.multiple_of(t * TILE, TILE), TILE, f), found)
    for taken, size in zip(short, TAILS):
        found = lax.cond(taken, lambda f, size=size: scores(steps, at_rest, size, f), lambda f: f, found)
    inverse = [1.0 / f[1] for f in found]
    dsum = [f[2] * i for f, i in zip(found, inverse)]
    dqt[...] = jnp.zeros_like(dqt)

    def grads(t, at, size):
        row = pl.multiple_of(stop - at - size + PAD, HALF)
        for i, (g, c) in enumerate(CHUNKS):
            sl = slice(c * LANES, (c + 1) * LANES)
            to = slice(i * LANES, (i + 1) * LANES)
            kt = ks[g, pl.ds(row, size), :]
            p = es[pl.ds(at, size), to] * (jnp.exp2(ms[t, 0:1, to] - found[i][0]) * inverse[i])
            ds = (p * (dps[pl.ds(at, size), to] - dsum[i]) * SCALE).astype(jnp.bfloat16)
            dv[g, pl.ds(row, size), :] += jnp.dot(
                p.astype(jnp.bfloat16), gst[g, sl, :], preferred_element_type=jnp.float32
            )
            dk[g, pl.ds(row, size), :] += jnp.dot(ds, qst[g, sl, :], preferred_element_type=jnp.float32)
            dqt[:, to] += lax.dot_general(kt, ds, (((0,), (0,)), ((), ())), preferred_element_type=jnp.float32)

    lax.fori_loop(0, steps, lambda t, _: grads(t, pl.multiple_of(t * TILE, TILE), TILE), None)

    for taken, size in zip(short, TAILS):
        pl.when(taken)(lambda size=size: grads(steps, at_rest, size))

    for g in range(HEADS):
        for layer in range(2):
            for h in range(0, QUERY_PER_KEY, 2):
                r = g * ROWS + (layer * QUERY_PER_KEY + h) * HALF
                col = (g * QUERY_PER_KEY + h) * HEAD
                x = dqt[:, r : r + 128].astype(jnp.bfloat16).T
                dqs[layer][:, col : col + HEAD] = x[:HALF]
                dqs[layer][:, col + HEAD : col + 2 * HEAD] = x[HALF:]


def kernel(place, spans, lens, *refs):
    own, other, gathered, outs, total, scratch = refs[:4], refs[4:8], refs[8], refs[9:13], refs[13], refs[14:]
    ks, vs, dk, dv = scratch[:4]
    step = pl.program_id(0)
    core, chip = place[0] & 1, place[0] >> 1

    def position(k, s):
        return spans[4 * k + 2 * (core if s < 2 else 1 - core) + s % 2]

    @pl.when(step == 0)
    def _():
        ks[:, :PAD, :] = jnp.zeros((HEADS, PAD, HEAD), jnp.bfloat16)
        vs[:, :PAD, :] = jnp.zeros((HEADS, PAD, HEAD), jnp.bfloat16)
        dk[...] = jnp.zeros_like(dk)
        dv[...] = jnp.zeros_like(dv)
        for k in range(CHIPS):
            for s in range(4):
                p = pl.multiple_of(position(k, s) * HALF + PAD, HALF)
                x = gathered[k, s * HALF : (s + 1) * HALF, :]
                for g in range(HEADS):
                    ks[g, pl.ds(p, HALF), :] = x[:, g * HEAD : (g + 1) * HEAD]
                    vs[g, pl.ds(p, HALF), :] = x[:, PART + g * HEAD : PART + (g + 1) * HEAD]

    first = spans[4 * chip + 2 * core + step]
    second = spans[4 * chip + 2 * (1 - core) + step]
    block_grads(first, lens, own[:2], own[2:], outs[:2], *scratch)
    block_grads(second, lens, other[:2], other[2:], outs[2:], *scratch)

    @pl.when(step == 1)
    def _():
        for k in range(CHIPS):
            for s in range(4):
                p = pl.multiple_of(position(k, s) * HALF + PAD, HALF)
                rows = slice(s * HALF, (s + 1) * HALF)
                for g in range(HEADS):
                    cols = slice(g * HEAD, (g + 1) * HEAD)
                    total[k, rows, cols] = dk[g, pl.ds(p, HALF), :].astype(jnp.bfloat16)
                    cols = slice(PART + g * HEAD, PART + (g + 1) * HEAD)
                    total[k, rows, cols] = dv[g, pl.ds(p, HALF), :].astype(jnp.bfloat16)


def chip_grads(g, place, spans, lens, own, other, gathered):
    by_core = pl.BlockSpec((HALF, HEADS * WIDTH), lambda s, place, *_: (s, (place[0] & 1) * SHARE + g))
    by_step = pl.BlockSpec((HALF, HEADS * WIDTH), lambda s, *_: (s, 0))
    all_chips = pl.BlockSpec((CHIPS, 4 * HALF, 2 * PART), lambda s, *_: (0, 0, 0))
    return pl.pallas_call(
        kernel,
        grid_spec=pltpu.PrefetchScalarGridSpec(
            num_scalar_prefetch=3,
            grid=(2,),
            in_specs=[by_core] * 8 + [all_chips],
            out_specs=[by_step] * 4 + [all_chips],
            scratch_shapes=[
                pltpu.VMEM((HEADS, TOKENS + PAD, HEAD), jnp.bfloat16),
                pltpu.VMEM((HEADS, TOKENS + PAD, HEAD), jnp.bfloat16),
                pltpu.VMEM((HEADS, TOKENS + PAD, HEAD), jnp.float32),
                pltpu.VMEM((HEADS, TOKENS + PAD, HEAD), jnp.float32),
                pltpu.VMEM((KEYS, HEADS * ROWS), jnp.float32),
                pltpu.VMEM((KEYS, HEADS * ROWS), jnp.float32),
                pltpu.VMEM((KEYS // TILE + 1, 8, HEADS * ROWS), jnp.float32),
                pltpu.VMEM((HEAD, HEADS * ROWS), jnp.float32),
                pltpu.VMEM((HEADS, ROWS, HEAD), jnp.bfloat16),
                pltpu.VMEM((HEADS, ROWS, HEAD), jnp.bfloat16),
                pltpu.VMEM((TILE, 128), jnp.float32),
            ],
        ),
        out_shape=[jax.ShapeDtypeStruct((2 * HALF, HEADS * WIDTH), jnp.bfloat16)] * 4
        + [jax.ShapeDtypeStruct((CHIPS, 4 * HALF, 2 * PART), jnp.bfloat16)],
        compiler_params=pltpu.CompilerParams(
            dimension_semantics=("arbitrary",), vmem_limit_bytes=60 * 2**20
        ),
        cost_estimate=pl.CostEstimate(flops=12 * 10**9, bytes_accessed=6 * 2**20, transcendentals=2 * 10**6),
        name="chip_grads",
    )(place, spans, lens, *own, *other, gathered)


def local(query_one, query_two, keys, values, cotangent_one, cotangent_two, span_order, lengths):
    device = lax.axis_index("ctx")
    core = device & 1

    def parts(who):
        k, v = [lax.dynamic_slice(x, (0, who * SHARE * HEAD), (2 * HALF, SHARE * HEAD)) for x in (keys, values)]
        return [x[:, g * HEAD : (g + 1) * HEAD] for g in range(SHARE) for x in (k, v)]

    theirs = swap(jnp.concatenate(parts(1 - core), axis=1))
    mine = parts(core)
    sent = []
    for g in range(SHARE):
        x = jnp.concatenate(mine[2 * g : 2 * g + 2], axis=1)
        x = jnp.concatenate([x, theirs[:, 2 * g * HEAD : (2 * g + 2) * HEAD]], axis=0)
        sent.append(jnp.broadcast_to(x, (CHIPS, *x.shape)))
    own = (query_one, query_two, cotangent_one, cotangent_two)
    own, sent[0] = lax.optimization_barrier((own, sent[0]))
    other = [swap(a) for a in own]
    place = jnp.reshape(device, (1,))
    grads, sums = [], []
    for g in range(SHARE):
        *dqs, total = chip_grads(g, place, span_order, lengths, own, other, exchange(sent[g]))
        grads.append(dqs)
        sums.append(jnp.sum(exchange(total).astype(jnp.float32), axis=0).astype(jnp.bfloat16))
    got = swap(jnp.concatenate([x[2 * HALF :] for x in sums], axis=1))
    kept = jnp.concatenate([x[: 2 * HALF] for x in sums], axis=1)

    def whole(a, b):
        return jnp.where(core == 0, jnp.concatenate(a + b, axis=1), jnp.concatenate(b + a, axis=1))

    def heads(x, k):
        return [x[:, (2 * g + k) * HEAD : (2 * g + k + 1) * HEAD] for g in range(SHARE)]

    return (
        whole([d[0] for d in grads], [swap(d[2]) for d in grads]),
        whole([d[1] for d in grads], [swap(d[3]) for d in grads]),
        whole(heads(kept, 0), heads(got, 0)),
        whole(heads(kept, 1), heads(got, 1)),
    )


def solution(mesh):
    rows = P(("dp", "ctx"), None)
    return jax.shard_map(
        local,
        mesh=mesh,
        in_specs=(rows,) * 6 + (P("dp"), P("dp")),
        out_specs=(rows,) * 4,
        check_vma=False,
    )
```

```python
import math

import jax
import jax.numpy as jnp
from jax import lax
from jax.experimental import pallas as pl
from jax.experimental.pallas import tpu as pltpu
from jax.sharding import PartitionSpec as P

HEAD = 128
KEY_VALUE_HEADS = 4
QUERY_PER_KEY = 8
HALF = 64
MOST = 1024
NEG = -1e30
SCALE = HEAD**-0.5
LOG2E = math.log2(math.e)
Z, Y = 4, 2
CHIPS = Z * Y
TOKENS = 2048
BLOCKS = TOKENS // HALF
SHARE = KEY_VALUE_HEADS // 2
HEADS = 1
PART = HEADS * HEAD
WIDTH = QUERY_PER_KEY * HEAD
ROWS = 2 * QUERY_PER_KEY * HALF
TILE = 512
TAILS = (128, 256, 384)
PAD = TILE
KEYS = (MOST + HALF + TAILS[0]) // TAILS[0] * TAILS[0]
LANES = 1024
CHUNKS = [(g, c) for g in range(HEADS) for c in range(ROWS // LANES)]


def device_of(z, y, core):
    return ((z % Z) * Y + y % Y) * 2 + core


def swap(x):
    return lax.ppermute(x, "ctx", [(d, d ^ 1) for d in range(CHIPS * 2)])


def exchange(x):
    groups = [[device_of(z, y, c) for z in range(Z) for y in range(Y)] for c in range(2)]
    return lax.all_to_all(x, "ctx", 0, 0, axis_index_groups=groups, tiled=True)


def block_grads(position, lens, qs, gs, dqs, ks, vs, dk, dv, es, dps, ms, dqt, qst, gst, bias):
    token = lax.broadcasted_iota(jnp.int32, (1, 128), 1) % HALF
    where = position * HALF + token
    starts = jnp.zeros((1, 128), jnp.int32)
    low = jnp.int32(0)
    end = jnp.int32(0)
    for k in range(lens.shape[0]):
        end = end + lens[k]
        starts = jnp.where(where >= end, end, starts)
        low = jnp.where(position * HALF >= end, end, low)
    stop = (position + 1) * HALF
    count = stop - low
    steps = (count + TILE - TAILS[-1] - 1) // TILE
    rest = count - steps * TILE
    short = [(low < rest) & (rest <= size) for low, size in zip((0, *TAILS), TAILS)]
    for g in range(HEADS):
        for layer in range(2):
            for h in range(QUERY_PER_KEY):
                r = (layer * QUERY_PER_KEY + h) * HALF
                col = (g * QUERY_PER_KEY + h) * HEAD
                qst[g, r : r + HALF, :] = qs[layer][:, col : col + HEAD]
                gst[g, r : r + HALF, :] = gs[layer][:, col : col + HEAD]
    by_head = (((1,), (1,)), ((), ()))

    def scores(t, at, size, carry):
        base = stop - at - size
        row = pl.multiple_of(base + PAD, HALF)
        key = base + lax.broadcasted_iota(jnp.int32, (size, 128), 0)
        bias[:size, :] = jnp.where((key <= where) & (key >= starts), 0.0, NEG)
        out = []
        for i, (g, c) in enumerate(CHUNKS):
            top, total, mean = carry[i]
            sl = slice(c * LANES, (c + 1) * LANES)
            to = slice(i * LANES, (i + 1) * LANES)
            kt = ks[g, pl.ds(row, size), :]
            vt = vs[g, pl.ds(row, size), :]
            s = lax.dot_general(kt, qst[g, sl, :], by_head, preferred_element_type=jnp.float32)
            dp = lax.dot_general(vt, gst[g, sl, :], by_head, preferred_element_type=jnp.float32)
            s = s * (SCALE * LOG2E) + jnp.concatenate([bias[:size, :]] * (LANES // 128), axis=1)
            now = jnp.maximum(top, jnp.max(s, axis=0, keepdims=True))
            e = jnp.exp2(s - now)
            shrink = jnp.exp2(top - now)
            total = total * shrink + jnp.sum(e, axis=0, keepdims=True)
            mean = mean * shrink + jnp.sum(e * dp, axis=0, keepdims=True)
            es[pl.ds(at, size), to] = e
            dps[pl.ds(at, size), to] = dp
            ms[t, :, to] = jnp.broadcast_to(now, (8, LANES))
            out.append((now, total, mean))
        return tuple(out)

    zero = jnp.zeros((1, LANES), jnp.float32)
    found = tuple((zero + NEG, zero, zero) for _ in CHUNKS)
    at_rest = pl.multiple_of(steps * TILE, TILE)
    found = lax.fori_loop(0, steps, lambda t, f: scores(t, pl.multiple_of(t * TILE, TILE), TILE, f), found)
    for taken, size in zip(short, TAILS):
        found = lax.cond(taken, lambda f, size=size: scores(steps, at_rest, size, f), lambda f: f, found)
    inverse = [1.0 / f[1] for f in found]
    dsum = [f[2] * i for f, i in zip(found, inverse)]
    dqt[...] = jnp.zeros_like(dqt)

    def grads(t, at, size):
        row = pl.multiple_of(stop - at - size + PAD, HALF)
        for i, (g, c) in enumerate(CHUNKS):
            sl = slice(c * LANES, (c + 1) * LANES)
            to = slice(i * LANES, (i + 1) * LANES)
            kt = ks[g, pl.ds(row, size), :]
            p = es[pl.ds(at, size), to] * (jnp.exp2(ms[t, 0:1, to] - found[i][0]) * inverse[i])
            ds = (p * (dps[pl.ds(at, size), to] - dsum[i]) * SCALE).astype(jnp.bfloat16)
            dv[g, pl.ds(row, size), :] += jnp.dot(
                p.astype(jnp.bfloat16), gst[g, sl, :], preferred_element_type=jnp.float32
            )
            dk[g, pl.ds(row, size), :] += jnp.dot(ds, qst[g, sl, :], preferred_element_type=jnp.float32)
            dqt[:, to] += lax.dot_general(kt, ds, (((0,), (0,)), ((), ())), preferred_element_type=jnp.float32)

    lax.fori_loop(0, steps, lambda t, _: grads(t, pl.multiple_of(t * TILE, TILE), TILE), None)

    for taken, size in zip(short, TAILS):
        pl.when(taken)(lambda size=size: grads(steps, at_rest, size))

    for g in range(HEADS):
        for layer in range(2):
            for h in range(0, QUERY_PER_KEY, 2):
                r = g * ROWS + (layer * QUERY_PER_KEY + h) * HALF
                col = (g * QUERY_PER_KEY + h) * HEAD
                x = dqt[:, r : r + 128].astype(jnp.bfloat16).T
                dqs[layer][:, col : col + HEAD] = x[:HALF]
                dqs[layer][:, col + HEAD : col + 2 * HEAD] = x[HALF:]


def kernel(place, spans, lens, *refs):
    own, other, gathered, outs, total, scratch = refs[:4], refs[4:8], refs[8], refs[9:13], refs[13], refs[14:]
    ks, vs, dk, dv = scratch[:4]
    step = pl.program_id(0)
    core, chip = place[0] & 1, place[0] >> 1

    def position(k, s):
        return spans[4 * k + 2 * (core if s < 2 else 1 - core) + s % 2]

    @pl.when(step == 0)
    def _():
        ks[:, :PAD, :] = jnp.zeros((HEADS, PAD, HEAD), jnp.bfloat16)
        vs[:, :PAD, :] = jnp.zeros((HEADS, PAD, HEAD), jnp.bfloat16)
        dk[...] = jnp.zeros_like(dk)
        dv[...] = jnp.zeros_like(dv)
        for k in range(CHIPS):
            for s in range(4):
                p = pl.multiple_of(position(k, s) * HALF + PAD, HALF)
                x = gathered[k, s * HALF : (s + 1) * HALF, :]
                for g in range(HEADS):
                    ks[g, pl.ds(p, HALF), :] = x[:, g * HEAD : (g + 1) * HEAD]
                    vs[g, pl.ds(p, HALF), :] = x[:, PART + g * HEAD : PART + (g + 1) * HEAD]

    first = spans[4 * chip + 2 * core + step]
    second = spans[4 * chip + 2 * (1 - core) + step]
    block_grads(first, lens, own[:2], own[2:], outs[:2], *scratch)
    block_grads(second, lens, other[:2], other[2:], outs[2:], *scratch)

    @pl.when(step == 1)
    def _():
        for k in range(CHIPS):
            for s in range(4):
                p = pl.multiple_of(position(k, s) * HALF + PAD, HALF)
                rows = slice(s * HALF, (s + 1) * HALF)
                for g in range(HEADS):
                    cols = slice(g * HEAD, (g + 1) * HEAD)
                    total[k, rows, cols] = dk[g, pl.ds(p, HALF), :].astype(jnp.bfloat16)
                    cols = slice(PART + g * HEAD, PART + (g + 1) * HEAD)
                    total[k, rows, cols] = dv[g, pl.ds(p, HALF), :].astype(jnp.bfloat16)


def chip_grads(g, place, spans, lens, own, other, gathered):
    by_core = pl.BlockSpec((HALF, HEADS * WIDTH), lambda s, place, *_: (s, (place[0] & 1) * SHARE + g))
    by_step = pl.BlockSpec((HALF, HEADS * WIDTH), lambda s, *_: (s, 0))
    all_chips = pl.BlockSpec((CHIPS, 4 * HALF, 2 * PART), lambda s, *_: (0, 0, 0))
    return pl.pallas_call(
        kernel,
        grid_spec=pltpu.PrefetchScalarGridSpec(
            num_scalar_prefetch=3,
            grid=(2,),
            in_specs=[by_core] * 8 + [all_chips],
            out_specs=[by_step] * 4 + [all_chips],
            scratch_shapes=[
                pltpu.VMEM((HEADS, TOKENS + PAD, HEAD), jnp.bfloat16),
                pltpu.VMEM((HEADS, TOKENS + PAD, HEAD), jnp.bfloat16),
                pltpu.VMEM((HEADS, TOKENS + PAD, HEAD), jnp.float32),
                pltpu.VMEM((HEADS, TOKENS + PAD, HEAD), jnp.float32),
                pltpu.VMEM((KEYS, HEADS * ROWS), jnp.float32),
                pltpu.VMEM((KEYS, HEADS * ROWS), jnp.float32),
                pltpu.VMEM((KEYS // TILE + 1, 8, HEADS * ROWS), jnp.float32),
                pltpu.VMEM((HEAD, HEADS * ROWS), jnp.float32),
                pltpu.VMEM((HEADS, ROWS, HEAD), jnp.bfloat16),
                pltpu.VMEM((HEADS, ROWS, HEAD), jnp.bfloat16),
                pltpu.VMEM((TILE, 128), jnp.float32),
            ],
        ),
        out_shape=[jax.ShapeDtypeStruct((2 * HALF, HEADS * WIDTH), jnp.bfloat16)] * 4
        + [jax.ShapeDtypeStruct((CHIPS, 4 * HALF, 2 * PART), jnp.bfloat16)],
        compiler_params=pltpu.CompilerParams(
            dimension_semantics=("arbitrary",), vmem_limit_bytes=60 * 2**20
        ),
        cost_estimate=pl.CostEstimate(flops=12 * 10**9, bytes_accessed=6 * 2**20, transcendentals=2 * 10**6),
        name="chip_grads",
    )(place, spans, lens, *own, *other, gathered)


def local(query_one, query_two, keys, values, cotangent_one, cotangent_two, span_order, lengths):
    device = lax.axis_index("ctx")
    core = device & 1

    def parts(who):
        k, v = [lax.dynamic_slice(x, (0, who * SHARE * HEAD), (2 * HALF, SHARE * HEAD)) for x in (keys, values)]
        return [x[:, g * HEAD : (g + 1) * HEAD] for g in range(SHARE) for x in (k, v)]

    theirs = swap(jnp.concatenate(parts(1 - core), axis=1))
    mine = parts(core)
    sent = []
    for g in range(SHARE):
        x = jnp.concatenate(mine[2 * g : 2 * g + 2], axis=1)
        x = jnp.concatenate([x, theirs[:, 2 * g * HEAD : (2 * g + 2) * HEAD]], axis=0)
        sent.append(jnp.broadcast_to(x, (CHIPS, *x.shape)))
    own = (query_one, query_two, cotangent_one, cotangent_two)
    own, sent[1] = lax.optimization_barrier((own, sent[1]))
    other = [swap(a) for a in own]
    place = jnp.reshape(device, (1,))
    grads, sums = [], []
    for g in range(SHARE):
        *dqs, total = chip_grads(g, place, span_order, lengths, own, other, exchange(sent[g]))
        grads.append(dqs)
        sums.append(jnp.sum(exchange(total).astype(jnp.float32), axis=0).astype(jnp.bfloat16))
    grads, sums[0] = lax.optimization_barrier((grads, sums[0]))
    got = swap(jnp.concatenate([x[2 * HALF :] for x in sums], axis=1))
    kept = jnp.concatenate([x[: 2 * HALF] for x in sums], axis=1)

    def whole(a, b):
        return jnp.where(core == 0, jnp.concatenate(a + b, axis=1), jnp.concatenate(b + a, axis=1))

    def heads(x, k):
        return [x[:, (2 * g + k) * HEAD : (2 * g + k + 1) * HEAD] for g in range(SHARE)]

    return (
        whole([d[0] for d in grads], [swap(d[2]) for d in grads]),
        whole([d[1] for d in grads], [swap(d[3]) for d in grads]),
        whole(heads(kept, 0), heads(got, 0)),
        whole(heads(kept, 1), heads(got, 1)),
    )


def solution(mesh):
    rows = P(("dp", "ctx"), None)
    return jax.shard_map(
        local,
        mesh=mesh,
        in_specs=(rows,) * 6 + (P("dp"), P("dp")),
        out_specs=(rows,) * 4,
        check_vma=False,
    )
```
